32 devices in a mesh: section: 4 (over x, core), patch: 4 (over z), tensor: 2 (over y).
Axes of the slice: x: 2, y: 2, z: 4, core: 2. Of those that a mesh axis runs over, the one named last changes fastest.
Arguments:
- forward_input: bfloat16 [4, 1024, 1024], P('section', 'patch', 'tensor'), may hold values from -6 to 6
- backward_input: bfloat16 [4, 1024, 1024], P('section', 'patch', 'tensor'), may hold values from -6 to 6
- cotangent: bfloat16 [4, 1024, 1024], P('section', 'patch', 'tensor'), may hold values from -6 to 6
- norm_gain: float32 [4, 1024], P('section'), may hold values from 0.1 to 1.9
- projection: bfloat16 [4, 3, 1024, 1024], P('section', None, None, 'tensor'), may hold values from -6 to 6
- output_weight: bfloat16 [4, 1024, 1024], P('section', 'tensor'), may hold values from -0.1875 to 0.1875
- neighbours: int32 [1024, 9], P('patch'), may hold values from 0 to 1023, as said below
Outputs:
- forward_output: bfloat16 [4, 1024, 1024], P('section', 'patch', 'tensor')
- backward_output: bfloat16 [4, 1024, 1024], P('section', 'patch', 'tensor')
- grad_projection: float32 [4, 3, 1024, 1024], P('section', None, 'patch', 'tensor')
- grad_output_weight: float32 [4, 1024, 1024], P('section', 'tensor', 'patch')
- grad_gain: float32 [4, 1024], P('section', 'tensor')
The draws below stay inside these ranges and needn't reach their ends.
Inputs may be any that keep to these rules, and one draw needn't show every extreme that they name: `neighbours`: row i lists 9 different pixels: i itself, and pixels whose index differs from i by at most 64 modulo 1024.
All inputs are finite; a program needn't handle non-finite values.
Results may differ from the reference program's by a relative error of at most 0.0091.
Values may be sent and summed in bfloat16 or wider, within the bound.
A program may use at most 128 MiB of HBM per device.

```python
import jax
import jax.numpy as jnp
from jax import lax

D = 1024
HEADS = 16
HEAD = 64
NEIGH = 9
HALO = 64
PIX_DEV = 256
TOKENS = 1024
N_SECTION = 4
N_PATCH = 4


def draw_projection(key, part):
    key = jax.random.fold_in(key, 11)
    noise = jax.random.normal(key, (N_SECTION, 3, D, D), jnp.float32) * D ** (-0.5)
    return jnp.clip(noise, -6.0, 6.0).astype(jnp.bfloat16)


def draw_neighbours(key, part):
    key = jax.random.fold_in(key, 5)
    total = PIX_DEV * N_PATCH
    choices_count = 2 * HALO
    ranks = jax.random.randint(key, (total, choices_count), 0, 2 ** 20) * choices_count
    ranks = ranks + jnp.arange(choices_count, dtype=jnp.int32)[None, :]
    picked = lax.top_k(ranks, NEIGH - 1)[1]
    offsets = jnp.where(picked < HALO, picked - HALO, picked - HALO + 1)
    offsets = jnp.concatenate([jnp.zeros((total, 1), jnp.int32), offsets.astype(jnp.int32)], axis=1)
    positions = jnp.arange(total, dtype=jnp.int32)[:, None]
    return jnp.mod(positions + offsets, total).astype(jnp.int32)


def steps_of(stream_key, extent, shards, low, high):
    level, own = 1.0, jax.random.fold_in(stream_key, 6)
    for axis_at, parts in shards:
        heights = jnp.exp(jax.random.uniform(jax.random.fold_in(own, axis_at), (parts,), jnp.float32, low / len(shards), high / len(shards)))
        level = level * jnp.repeat(heights, extent[axis_at] // parts).reshape([-1 if axis == axis_at else 1 for axis in range(len(extent))])
    return level


def bell_draw(rng, shape, deviation, bound, cuts=(), kind=jnp.bfloat16):
    result = jax.random.normal(rng, shape, jnp.float32) * deviation
    if len(cuts) > 0:
        result = steps_of(rng, shape, cuts, -0.22, 0.18) * result
    return jnp.clip(result, min=-bound, max=bound).astype(kind)


def setup_inputs(seed: int = 0) -> dict:
    keys = jax.random.split(jax.random.key(seed), 8)
    forward_input = bell_draw(keys[0], (N_SECTION, TOKENS, D), 1.0, 6.0, ((0, 4), (1, 4), (2, 2)))
    backward_input = bell_draw(keys[1], (N_SECTION, TOKENS, D), 1.0, 6.0, ((0, 4), (1, 4), (2, 2)))
    cotangent = bell_draw(keys[2], (N_SECTION, TOKENS, D), 1.0, 6.0, ((0, 4), (1, 4), (2, 2)))
    norm_gain = jnp.clip(1.0 + 0.18 * jax.random.normal(keys[3], (N_SECTION, D), jnp.float32), 0.1, 1.9)
    projection = draw_projection(jax.random.fold_in(keys[7], 71), 0)
    output_weight = bell_draw(keys[5], (N_SECTION, D, D), D ** -0.5, 0.1875, ((0, 4), (1, 2)))
    neighbours = draw_neighbours(jax.random.fold_in(keys[7], 71), 0)
    return {"forward_input": forward_input, "backward_input": backward_input, "cotangent": cotangent, "norm_gain": norm_gain, "projection": projection, "output_weight": output_weight, "neighbours": neighbours}


EPSILON = 1e-06

def round_trip(values):
    return lax.optimization_barrier(values.astype(jnp.bfloat16)).astype(jnp.float32)

def normalize(inputs, gain):
    widened = inputs.astype(jnp.float32)
    inverse = lax.rsqrt(lax.optimization_barrier(jnp.mean(widened * widened, axis=-1, keepdims=True)) + EPSILON)
    unit_rows = widened * inverse
    normed = (unit_rows * gain).astype(jnp.bfloat16)
    return (inverse, unit_rows, normed)

def streams_of(normed, projection):
    query_all = jnp.dot(normed, projection[0], preferred_element_type=jnp.float32).astype(jnp.bfloat16)
    key_all = jnp.dot(normed, projection[1], preferred_element_type=jnp.float32).astype(jnp.bfloat16)
    value_all = jnp.dot(normed, projection[2], preferred_element_type=jnp.float32).astype(jnp.bfloat16)
    return (query_all, key_all, value_all)

def attend(query_rows, key_all, value_all, index_rows):
    block_rows = query_rows.shape[0]
    queries = query_rows.reshape(block_rows, HEADS, HEAD).astype(jnp.float32)
    near_keys = key_all[index_rows].reshape(block_rows, NEIGH, HEADS, HEAD).astype(jnp.float32)
    near_values = value_all[index_rows].reshape(block_rows, NEIGH, HEADS, HEAD).astype(jnp.float32)
    scores = jnp.einsum('bhe,bkhe->bhk', queries, near_keys) * HEAD ** (-0.5)
    maximum = lax.optimization_barrier(jnp.max(scores, axis=-1, keepdims=True))
    exponent = jnp.exp(scores - maximum)
    weights = exponent / lax.optimization_barrier(jnp.sum(exponent, axis=-1, keepdims=True))
    rounded = round_trip(weights)
    attended = jnp.einsum('bhk,bkhe->bhe', rounded, near_values).reshape(block_rows, HEADS * HEAD).astype(jnp.bfloat16)
    return (queries, near_keys, near_values, weights, rounded, attended)

def section_forward(inputs, gain, projection, output_weight, neighbours):
    inverse, unit_rows, normed = normalize(inputs, gain)
    query_all, key_all, value_all = streams_of(normed, projection)

    def one_block(pieces):
        return attend(pieces[0], key_all, value_all, pieces[1])[5]
    attended = lax.map(one_block, (query_all.reshape(N_PATCH, PIX_DEV, D), neighbours.reshape(N_PATCH, PIX_DEV, NEIGH)))
    attended = attended.reshape(N_PATCH * PIX_DEV, D)
    update = jnp.dot(attended, output_weight, preferred_element_type=jnp.float32)
    return (inputs.astype(jnp.float32) + update).astype(jnp.bfloat16)

def section_backward(inputs, upstream, gain, projection, output_weight, neighbours):
    total = N_PATCH * PIX_DEV
    inverse, unit_rows, normed = normalize(inputs, gain)
    query_all, key_all, value_all = streams_of(normed, projection)
    grad_attended = jnp.dot(upstream, output_weight.T, preferred_element_type=jnp.float32).astype(jnp.bfloat16)

    def one_block(carry, pieces):
        key_grad, value_grad = carry
        query_rows, index_rows, grad_rows = pieces
        queries, near_keys, near_values, weights, rounded, attended = attend(query_rows, key_all, value_all, index_rows)
        grad_heads = grad_rows.reshape(PIX_DEV, HEADS, HEAD).astype(jnp.float32)
        grad_weights = jnp.einsum('bhe,bkhe->bhk', grad_heads, near_values)
        grad_scores = weights * (grad_weights - lax.optimization_barrier(jnp.sum(weights * grad_weights, axis=-1, keepdims=True)))
        grad_scores = round_trip(grad_scores * HEAD ** (-0.5))
        query_grad = jnp.einsum('bhk,bkhe->bhe', grad_scores, near_keys).reshape(PIX_DEV, D)
        flat_index = index_rows.reshape(-1)
        key_terms = jnp.einsum('bhk,bhe->bkhe', grad_scores, queries).reshape(PIX_DEV * NEIGH, D)
        value_terms = jnp.einsum('bhk,bhe->bkhe', rounded, grad_heads).reshape(PIX_DEV * NEIGH, D)
        key_grad = key_grad + jax.ops.segment_sum(key_terms, flat_index, num_segments=total)
        value_grad = value_grad + jax.ops.segment_sum(value_terms, flat_index, num_segments=total)
        return ((key_grad, value_grad), (attended, query_grad))
    zeros = jnp.zeros((total, D), jnp.float32)
    pieces = (query_all.reshape(N_PATCH, PIX_DEV, D), neighbours.reshape(N_PATCH, PIX_DEV, NEIGH), grad_attended.reshape(N_PATCH, PIX_DEV, D))
    (key_grad, value_grad), (attended, query_grad) = lax.scan(one_block, (zeros, zeros), pieces)
    attended = attended.reshape(total, D)
    grads = [query_grad.reshape(total, D).astype(jnp.bfloat16), key_grad.astype(jnp.bfloat16), value_grad.astype(jnp.bfloat16)]
    grad_normed = jnp.zeros((total, D), jnp.float32)
    for stream in range(3):
        grad_normed = grad_normed + jnp.dot(grads[stream], projection[stream].T, preferred_element_type=jnp.float32)
    grad_projection = jnp.stack([jnp.dot(normed.T, grads[stream], preferred_element_type=jnp.float32) for stream in range(3)])
    grad_output = jnp.dot(attended.T, upstream, preferred_element_type=jnp.float32)
    grad_gain = lax.optimization_barrier(jnp.sum(grad_normed * unit_rows, axis=0))
    scaled = grad_normed * gain
    correction = lax.optimization_barrier(jnp.mean(scaled * unit_rows, axis=-1, keepdims=True))
    grad_inputs = upstream.astype(jnp.float32) + inverse * (scaled - unit_rows * correction)
    return (grad_inputs.astype(jnp.bfloat16), grad_projection, grad_output, grad_gain)

def reference(forward_input, backward_input, cotangent, norm_gain, projection, output_weight, neighbours):
    forward_list, backward_list, projection_list, output_list, gain_list = ([], [], [], [], [])
    for section in range(N_SECTION):
        forward_list.append(section_forward(forward_input[section], norm_gain[section], projection[section], output_weight[section], neighbours))
        grad_inputs, grad_projection, grad_output, grad_gain = section_backward(backward_input[section], cotangent[section], norm_gain[section], projection[section], output_weight[section], neighbours)
        backward_list.append(grad_inputs)
        projection_list.append(grad_projection)
        output_list.append(grad_output)
        gain_list.append(grad_gain)
    forward_output = jnp.roll(jnp.stack(forward_list), 1, axis=0)
    backward_output = jnp.roll(jnp.stack(backward_list), -1, axis=0)
    return (forward_output, backward_output, jnp.stack(projection_list), jnp.stack(output_list), jnp.stack(gain_list))
```

```python
import functools

import jax
import jax.numpy as jnp
from jax import lax
from jax.experimental import pallas as pl
from jax.experimental.pallas import tpu as pltpu
from jax.sharding import PartitionSpec as P

HEAD = 64
HALO = 64
TILE = 128
WINDOW = TILE + 2 * HALO
EPSILON = 1e-06
MESH = pl.DeviceIdType.MESH
F32 = jnp.float32
BF16 = jnp.bfloat16


def mm(a, b):
    return lax.dot_general(a, b, (((1,), (0,)), ((), ())), preferred_element_type=F32)


def mm_nt(a, b):
    return lax.dot_general(a, b, (((1,), (1,)), ((), ())), preferred_element_type=F32)


def mm_tn(a, b):
    return lax.dot_general(a, b, (((0,), (0,)), ((), ())), preferred_element_type=F32)


def kernel(
    n_section, n_patch, turned,
    xf_hbm, xb_hbm, cot_hbm, gain_ref, w_hbm, wo_hbm, near_ref,
    fo_ref, bo_ref, gp_ref, go_ref, gg_ref,
    xf, xb, cot, w, wo, bias, normed_b, normed_f, inverse_ref,
    q_b, q_f, kv_b, kv_f, g, att_b, att_f, grads, kvg, rim_out, rim_in,
    up_own, up_out, up_in, gn_own, gn_out, gn_in, corr_out, corr_in,
    fo_out, bo_out, parts, landed, gain_out, gain_in,
    loc, ts, tr, hs, hr, ss, sr, ws, wr, gs, gr,
):
    s, p, t = lax.axis_index("section"), lax.axis_index("patch"), lax.axis_index("tensor")
    peer = 1 - t
    rows, half = xf_hbm.shape
    width = 2 * half
    chunk = width // n_patch
    total = rows * n_patch
    after = lax.rem(p + 1, n_patch)
    before = lax.rem(p + n_patch - 1, n_patch)
    s_next = lax.rem(s + 1, n_section)
    s_prev = lax.rem(s + n_section - 1, n_section)

    w_copies = [pltpu.make_async_copy(w_hbm.at[c], w.at[c], loc.at[c]) for c in range(3)]
    wo_copy = pltpu.make_async_copy(wo_hbm, wo, loc.at[3])
    xb_copy = pltpu.make_async_copy(xb_hbm, xb.at[t], loc.at[4])
    cot_copy = pltpu.make_async_copy(cot_hbm, cot.at[t], loc.at[5])
    xf_copy = pltpu.make_async_copy(xf_hbm, xf.at[t], loc.at[6])
    for copy in (xb_copy, w_copies[1], w_copies[2], w_copies[0], cot_copy, wo_copy, xf_copy):
        copy.start()

    barrier = pltpu.get_barrier_semaphore()
    pl.semaphore_signal(barrier, inc=1, device_id={"tensor": peer}, device_id_type=MESH)
    pl.semaphore_signal(barrier, inc=1, device_id={"section": s_next}, device_id_type=MESH)
    pl.semaphore_signal(barrier, inc=1, device_id={"section": s_prev}, device_id_type=MESH)

    def greet(k, carry):
        pl.semaphore_signal(
            barrier, inc=1, device_id={"patch": lax.rem(p + k, n_patch)}, device_id_type=MESH
        )
        return carry

    lax.fori_loop(1, n_patch, greet, 0)
    pl.semaphore_wait(barrier, 2 + n_patch)

    def to_peer(i, src, dst):
        return pltpu.make_async_remote_copy(
            src_ref=src, dst_ref=dst, send_sem=ts.at[i], recv_sem=tr.at[i],
            device_id={"tensor": peer}, device_id_type=MESH,
        )

    def to_patch(i, src, dst, where):
        return pltpu.make_async_remote_copy(
            src_ref=src, dst_ref=dst, send_sem=hs.at[i], recv_sem=hr.at[i],
            device_id={"patch": where}, device_id_type=MESH,
        )

    xb_send = to_peer(0, xb_hbm, xb.at[t])
    cot_send = to_peer(1, cot_hbm, cot.at[t])
    xf_send = to_peer(2, xf_hbm, xf.at[t])
    xb_send.start()
    cot_send.start()
    xf_send.start()

    first = p * rows - HALO
    tile_start = lax.broadcasted_iota(jnp.int32, (rows, 1), 0) // TILE * TILE
    place = near_ref[...] - first
    place = jnp.where(place < 0, place + total, place)
    place = jnp.where(place >= total, place - total, place) - tile_start
    column = lax.broadcasted_iota(jnp.int32, (rows, WINDOW), 1)
    seen = jnp.full((rows, WINDOW), -1e30, F32)
    for k in range(near_ref.shape[1]):
        seen = jnp.where(place[:, k : k + 1] == column, 0.0, seen)
    bias[...] = seen

    def normalize(x, normed):
        lo, hi = x[0].astype(F32), x[1].astype(F32)
        square = jnp.sum(lo * lo, axis=-1, keepdims=True) + jnp.sum(hi * hi, axis=-1, keepdims=True)
        inverse = lax.rsqrt(square * (1.0 / width) + EPSILON)
        normed[:, :half] = (lo * inverse * gain_ref[0]).astype(BF16)
        normed[:, half:] = (hi * inverse * gain_ref[1]).astype(BF16)
        return inverse

    def key_value(normed, kv):
        kv[HALO : HALO + rows, :half] = mm(normed[...], w[1]).astype(BF16)
        kv[HALO : HALO + rows, half:] = mm(normed[...], w[2]).astype(BF16)

    def halo(i, kv):
        return (
            to_patch(i, kv.at[pl.ds(HALO, HALO)], kv.at[pl.ds(HALO + rows, HALO)], before),
            to_patch(i + 1, kv.at[pl.ds(rows, HALO)], kv.at[pl.ds(0, HALO)], after),
        )

    xb_copy.wait()
    xb_send.wait_recv()
    inverse_ref[...] = jnp.broadcast_to(normalize(xb, normed_b), inverse_ref.shape)
    w_copies[1].wait()
    w_copies[2].wait()
    key_value(normed_b, kv_b)
    halo_b = halo(0, kv_b)
    for copy in halo_b:
        copy.start()
    w_copies[0].wait()
    q_b[...] = mm(normed_b[...], w[0]).astype(BF16)

    cot_copy.wait()
    wo_copy.wait()
    cot_send.wait_recv()
    g[...] = (mm_nt(cot[0], wo[:, :half]) + mm_nt(cot[1], wo[:, half:])).astype(BF16)

    xf_copy.wait()
    xf_send.wait_recv()
    normalize(xf, normed_f)
    key_value(normed_f, kv_f)
    halo_f = halo(2, kv_f)
    for copy in halo_f:
        copy.start()
    q_f[...] = mm(normed_f[...], w[0]).astype(BF16)

    lane = lax.broadcasted_iota(jnp.int32, (TILE, 2 * HEAD), 1)
    is_low = lane < HEAD
    low = jnp.where(is_low, 1.0, 0.0).astype(BF16)
    high = jnp.where(is_low, 0.0, 1.0).astype(BF16)

    def stacked(x):
        return jnp.concatenate([x * low, x * high], axis=0)

    def unstacked(x):
        return jnp.where(is_low, x[:TILE], x[TILE:])

    pairs = half // (2 * HEAD)
    steps = rows // TILE * pairs
    scale = HEAD ** (-0.5)

    def places(step):
        row = pl.multiple_of(step // pairs * TILE, TILE)
        col = pl.multiple_of(lax.rem(step, pairs) * (2 * HEAD), 2 * HEAD)
        value_col = pl.multiple_of(half + lax.rem(step, pairs) * (2 * HEAD), 2 * HEAD)
        return row, col, value_col

    def weights_of(q, kv, row, col):
        queries = stacked(q[pl.ds(row, TILE), pl.ds(col, 2 * HEAD)])
        keys = kv[pl.ds(row, WINDOW), pl.ds(col, 2 * HEAD)]
        mask = bias[pl.ds(row, TILE), :]
        scores = mm_nt(queries, keys) * scale + jnp.concatenate([mask, mask], axis=0)
        exponent = jnp.exp(scores - jnp.max(scores, axis=-1, keepdims=True))
        weights = exponent * (1.0 / jnp.sum(exponent, axis=-1, keepdims=True))
        return queries, keys, weights

    for copy in halo_b:
        copy.wait_recv()
    kvg[...] = jnp.zeros_like(kvg)

    def backward_step(step, carry):
        row, col, value_col = places(step)
        queries, keys, weights = weights_of(q_b, kv_b, row, col)
        values = kv_b[pl.ds(row, WINDOW), pl.ds(value_col, 2 * HEAD)]
        rounded = weights.astype(BF16)
        here = (pl.ds(row, TILE), pl.ds(col, 2 * HEAD))
        att_b[here] = unstacked(mm(rounded, values)).astype(BF16)
        grad_heads = stacked(g[here])
        grad_weights = mm_nt(grad_heads, values)
        inner = jnp.sum(weights * grad_weights, axis=-1, keepdims=True)
        grad_scores = (weights * (grad_weights - inner) * scale).astype(BF16)
        grads[0, pl.ds(row, TILE), pl.ds(col, 2 * HEAD)] = unstacked(mm(grad_scores, keys)).astype(BF16)
        kvg[pl.ds(row, WINDOW), pl.ds(col, 2 * HEAD)] += mm_tn(grad_scores, queries)
        kvg[pl.ds(row, WINDOW), pl.ds(value_col, 2 * HEAD)] += mm_tn(rounded, grad_heads)
        return carry

    lax.fori_loop(0, steps, backward_step, 0)

    rim_out[0] = kvg[:HALO].astype(BF16)
    rim_out[1] = kvg[HALO + rows :].astype(BF16)
    rims = (
        to_patch(4, rim_out.at[0], rim_in.at[0], before),
        to_patch(5, rim_out.at[1], rim_in.at[1], after),
    )
    for copy in rims:
        copy.start()

    def part_copy(i, k):
        where = lax.rem(p + k, n_patch)
        return pltpu.make_async_remote_copy(
            src_ref=parts.at[i, pl.ds(pl.multiple_of(where * chunk, chunk), chunk)],
            dst_ref=landed.at[i, k], send_sem=ws.at[i, k], recv_sem=wr.at[i, k],
            device_id={"patch": where}, device_id_type=MESH,
        )

    def send_part(i):
        def one(k, carry):
            part_copy(i, k).start()
            return carry

        lax.fori_loop(1, n_patch, one, 0)

    parts[0, :half] = mm_tn(cot[0], att_b[...]).astype(BF16)
    parts[0, half:] = mm_tn(cot[1], att_b[...]).astype(BF16)
    send_part(0)
    parts[1] = mm_tn(normed_b[...], grads[0]).astype(BF16)
    send_part(1)

    for copy in halo_f:
        copy.wait_recv()

    def forward_step(step, carry):
        row, col, value_col = places(step)
        weights = weights_of(q_f, kv_f, row, col)[2]
        values = kv_f[pl.ds(row, WINDOW), pl.ds(value_col, 2 * HEAD)]
        att_f[pl.ds(row, TILE), pl.ds(col, 2 * HEAD)] = unstacked(
            mm(weights.astype(BF16), values)
        ).astype(BF16)
        return carry

    def forward_half(which):
        return mm(att_f[...], wo[:, pl.ds(pl.multiple_of(which * half, half), half)])

    for copy in rims:
        copy.wait_recv()
    kvg[pl.ds(rows, HALO)] += rim_in[0].astype(F32)
    kvg[pl.ds(HALO, HALO)] += rim_in[1].astype(F32)
    grads[1] = kvg[HALO : HALO + rows, :half].astype(BF16)
    grads[2] = kvg[HALO : HALO + rows, half:].astype(BF16)
    parts[2] = mm_tn(normed_b[...], grads[1]).astype(BF16)
    send_part(2)
    parts[3] = mm_tn(normed_b[...], grads[2]).astype(BF16)
    send_part(3)

    inverse = inverse_ref[:, :1]

    def normed_half(which):
        d = pl.ds(pl.multiple_of(which * half, half), half)
        return mm_nt(grads[0], w[0, d]) + mm_nt(grads[1], w[1, d]) + mm_nt(grads[2], w[2, d])

    def unit_half(which):
        return xb[which].astype(F32) * inverse

    away = normed_half(peer)
    gn_out[...] = away.astype(BF16)
    gn_send = to_peer(4, gn_out, gn_in)
    gn_send.start()
    near = normed_half(t)
    gn_own[...] = near
    corr = jnp.sum(away * unit_half(peer) * gain_ref[peer], axis=-1, keepdims=True)
    corr = corr + jnp.sum(near * unit_half(t) * gain_ref[t], axis=-1, keepdims=True)
    corr_row = jnp.broadcast_to(corr, (rows, 128)).T
    corr_out[...] = corr_row[:8]
    corr_send = to_peer(5, corr_out, corr_in)
    corr_send.start()

    lax.fori_loop(0, steps, forward_step, 0)
    up_out[...] = forward_half(peer).astype(BF16)
    up_send = to_peer(3, up_out, up_in)
    up_send.start()
    up_own[...] = forward_half(t)

    gn_send.wait_recv()
    corr_send.wait_recv()
    summed = gn_own[...] + gn_in[...].astype(F32)
    unit = unit_half(t)
    row_sum = jnp.broadcast_to((corr_out[...] + corr_in[...])[:1], (128, rows)).T[:, :1]
    change = inverse * (summed * gain_ref[t] - unit * (row_sum * (1.0 / width)))
    bo_out[...] = (cot[t].astype(F32) + change).astype(BF16)
    bo_send = pltpu.make_async_remote_copy(
        src_ref=bo_out, dst_ref=bo_ref, send_sem=ss.at[0], recv_sem=sr.at[0],
        device_id={"section": s_prev}, device_id_type=MESH,
    )
    bo_send.start()
    gain_own = jnp.sum(summed * unit, axis=0, keepdims=True)
    gain_out[...] = jnp.broadcast_to(gain_own, gain_out.shape)

    def gain_copy(k):
        return pltpu.make_async_remote_copy(
            src_ref=gain_out, dst_ref=gain_in.at[k], send_sem=gs.at[k], recv_sem=gr.at[k],
            device_id={"patch": lax.rem(p + k, n_patch)}, device_id_type=MESH,
        )

    def gain_start(k, carry):
        gain_copy(k).start()
        return carry

    lax.fori_loop(1, n_patch, gain_start, 0)

    up_send.wait_recv()
    fo_out[...] = (xf[t].astype(F32) + up_own[...] + up_in[...].astype(F32)).astype(BF16)
    fo_send = pltpu.make_async_remote_copy(
        src_ref=fo_out, dst_ref=fo_ref, send_sem=ss.at[1], recv_sem=sr.at[1],
        device_id={"section": s_next}, device_id_type=MESH,
    )
    fo_send.start()

    def gain_end(k, total_gain):
        copy = gain_copy(k)
        copy.wait_send()
        copy.wait_recv()
        return total_gain + gain_in[k]

    gg_ref[...] = lax.fori_loop(1, n_patch, gain_end, gain_out[...])

    own = pl.ds(pl.multiple_of(p * chunk, chunk), chunk)
    for i in range(4):
        def part_end(k, total_part):
            copy = part_copy(i, k)
            copy.wait_send()
            copy.wait_recv()
            gp_ref_i[...] += landed[i, k].astype(F32)
            return total_part

        gp_ref_i = gp_ref.at[i - 1] if i > 0 else (gn_own.at[pl.ds(0, chunk)] if turned else go_ref)
        gp_ref_i[...] = parts[i, own].astype(F32)
        lax.fori_loop(1, n_patch, part_end, 0)
    if turned:
        go_ref[...] = gn_own[:chunk].T

    for copy in (xb_send, cot_send, xf_send, gn_send, corr_send, up_send):
        copy.wait_send()
    for copy in halo_b + halo_f + rims:
        copy.wait_send()
    bo_send.wait()
    fo_send.wait()


def shards(n_section, n_patch, xf, xb, cot, norm_gain, projection, output_weight, neighbours):
    rows, half = xf.shape[1:]
    width = 2 * half
    chunk = width // n_patch
    turned = chunk % 128 == 0
    anywhere = pl.BlockSpec(memory_space=pl.ANY)
    vmem = pl.BlockSpec(memory_space=pltpu.VMEM)
    block = lambda *shape, dtype=BF16: pltpu.VMEM(shape, dtype)
    dma = pltpu.SemaphoreType.DMA
    outs = pl.pallas_call(
        functools.partial(kernel, n_section, n_patch, turned),
        out_shape=(
            jax.ShapeDtypeStruct((rows, half), BF16),
            jax.ShapeDtypeStruct((rows, half), BF16),
            jax.ShapeDtypeStruct((3, chunk, half), F32),
            jax.ShapeDtypeStruct((half, chunk) if turned else (chunk, half), F32),
            jax.ShapeDtypeStruct((8, half), F32),
        ),
        in_specs=[anywhere, anywhere, anywhere, vmem, anywhere, anywhere, vmem],
        out_specs=(anywhere, anywhere, vmem, vmem, vmem),
        scratch_shapes=[
            block(2, rows, half), block(2, rows, half), block(2, rows, half),
            block(3, width, half), block(half, width), block(rows, WINDOW, dtype=F32),
            block(rows, width), block(rows, width), block(rows, 128, dtype=F32),
            block(rows, half), block(rows, half),
            block(rows + 2 * HALO, width), block(rows + 2 * HALO, width),
            block(rows, half), block(rows, half), block(rows, half), block(3, rows, half),
            block(rows + 2 * HALO, width, dtype=F32), block(2, HALO, width), block(2, HALO, width),
            block(rows, half, dtype=F32), block(rows, half), block(rows, half),
            block(rows, half, dtype=F32), block(rows, half), block(rows, half),
            block(8, rows, dtype=F32), block(8, rows, dtype=F32),
            block(rows, half), block(rows, half),
            block(4, width, half), block(4, n_patch, chunk, half),
            block(8, half, dtype=F32), block(n_patch, 8, half, dtype=F32),
            dma((7,)), dma((6,)), dma((6,)), dma((6,)), dma((6,)), dma((2,)), dma((2,)),
            dma((4, n_patch)), dma((4, n_patch)), dma((n_patch,)), dma((n_patch,)),
        ],
        compiler_params=pltpu.CompilerParams(
            collective_id=0, has_side_effects=True, vmem_limit_bytes=56 * 2**20
        ),
        cost_estimate=pl.CostEstimate(flops=6 * 10**9, bytes_accessed=8 * 2**20, transcendentals=10**6),
    )(
        xf[0], xb[0], cot[0], norm_gain[0].reshape(2, 1, half), projection[0], output_weight[0],
        neighbours,
    )
    forward, backward, grad_projection, grad_output, gain = outs
    if not turned:
        grad_output = grad_output.T
    return forward[None], backward[None], grad_projection[None], grad_output[None], gain[:1]


def solution(mesh):
    return jax.shard_map(
        functools.partial(shards, mesh.shape["section"], mesh.shape["patch"]),
        mesh=mesh,
        in_specs=(
            P("section", "patch", "tensor"),
            P("section", "patch", "tensor"),
            P("section", "patch", "tensor"),
            P("section", None),
            P("section", None, None, "tensor"),
            P("section", "tensor", None),
            P("patch", None),
        ),
        out_specs=(
            P("section", "patch", "tensor"),
            P("section", "patch", "tensor"),
            P("section", None, "patch", "tensor"),
            P("section", "tensor", "patch"),
            P("section", "tensor"),
        ),
        check_vma=False,
    )
```

```python
import functools

import jax
import jax.numpy as jnp
from jax import lax
from jax.experimental import pallas as pl
from jax.experimental.pallas import tpu as pltpu
from jax.sharding import PartitionSpec as P

HEAD = 64
HALO = 64
TILE = 128
WINDOW = TILE + 2 * HALO
EPSILON = 1e-06
MESH = pl.DeviceIdType.MESH
F32 = jnp.float32
BF16 = jnp.bfloat16


def mm(a, b):
    return lax.dot_general(a, b, (((1,), (0,)), ((), ())), preferred_element_type=F32)


def mm_nt(a, b):
    return lax.dot_general(a, b, (((1,), (1,)), ((), ())), preferred_element_type=F32)


def mm_tn(a, b):
    return lax.dot_general(a, b, (((0,), (0,)), ((), ())), preferred_element_type=F32)


def kernel(
    n_section, n_patch, turned,
    xf_hbm, xb_hbm, cot_hbm, gain_ref, w_hbm, wo_hbm, near_ref,
    fo_ref, bo_ref, gp_ref, go_ref, gg_ref,
    xf, xb, cot, w, wo, bias, normed_b, normed_f, inverse_ref,
    q_b, q_f, kv_b, kv_f, g, att_b, att_f, grad_q, kvg, rim_out, rim_in,
    up_own, up_out, up_in, gn_own, gn_out, gn_in, corr_out, corr_in,
    fo_out, bo_out, parts, landed, gain_out, gain_in, near, turned_b, columns, gathered,
    loc, ts, tr, hs, hr, ss, sr, rs_s, rs_r, ag_s, ag_r, ns, nr, gs, gr,
):
    s, p, t = lax.axis_index("section"), lax.axis_index("patch"), lax.axis_index("tensor")
    peer = 1 - t
    rows, half = xf_hbm.shape
    width = 2 * half
    chunk = width // n_patch
    total = rows * n_patch
    after = lax.rem(p + 1, n_patch)
    before = lax.rem(p + n_patch - 1, n_patch)
    s_next = lax.rem(s + 1, n_section)
    s_prev = lax.rem(s + n_section - 1, n_section)

    w_copies = [pltpu.make_async_copy(w_hbm.at[c], w.at[c], loc.at[c]) for c in range(3)]
    wo_copy = pltpu.make_async_copy(wo_hbm, wo, loc.at[3])
    xb_copy = pltpu.make_async_copy(xb_hbm, xb.at[t], loc.at[4])
    cot_copy = pltpu.make_async_copy(cot_hbm, cot.at[t], loc.at[5])
    xf_copy = pltpu.make_async_copy(xf_hbm, xf.at[t], loc.at[6])
    for copy in (xb_copy, w_copies[1], w_copies[2], w_copies[0], cot_copy, wo_copy, xf_copy):
        copy.start()

    barrier = pltpu.get_barrier_semaphore()
    pl.semaphore_signal(barrier, inc=1, device_id={"tensor": peer}, device_id_type=MESH)
    pl.semaphore_signal(barrier, inc=1, device_id={"section": s_next}, device_id_type=MESH)
    pl.semaphore_signal(barrier, inc=1, device_id={"section": s_prev}, device_id_type=MESH)

    def greet(k, carry):
        pl.semaphore_signal(
            barrier, inc=1, device_id={"patch": lax.rem(p + k, n_patch)}, device_id_type=MESH
        )
        return carry

    lax.fori_loop(1, n_patch, greet, 0)
    pl.semaphore_wait(barrier, 2 + n_patch)

    def to_peer(i, src, dst):
        return pltpu.make_async_remote_copy(
            src_ref=src, dst_ref=dst, send_sem=ts.at[i], recv_sem=tr.at[i],
            device_id={"tensor": peer}, device_id_type=MESH,
        )

    def to_patch(i, src, dst, where):
        return pltpu.make_async_remote_copy(
            src_ref=src, dst_ref=dst, send_sem=hs.at[i], recv_sem=hr.at[i],
            device_id={"patch": where}, device_id_type=MESH,
        )

    xb_send = to_peer(0, xb_hbm, xb.at[t])
    cot_send = to_peer(1, cot_hbm, cot.at[t])
    xf_send = to_peer(2, xf_hbm, xf.at[t])
    xb_send.start()

    first = p * rows - HALO
    tile_start = lax.broadcasted_iota(jnp.int32, (rows, 1), 0) // TILE * TILE
    near[...] = jnp.zeros_like(near)
    near[: near_ref.shape[0], :] = near_ref[...].astype(F32)
    place = near[...].T.astype(jnp.int32) - first
    place = jnp.where(place < 0, place + total, place)
    place = jnp.where(place >= total, place - total, place) - tile_start
    column = lax.broadcasted_iota(jnp.int32, (rows, WINDOW), 1)
    seen = jnp.full((rows, WINDOW), -1e30, F32)
    for k in range(near_ref.shape[0]):
        seen = jnp.where(place[:, k : k + 1] == column, 0.0, seen)
    bias[...] = seen

    def normalize(x, normed):
        lo, hi = x[0].astype(F32), x[1].astype(F32)
        square = jnp.sum(lo * lo, axis=-1, keepdims=True) + jnp.sum(hi * hi, axis=-1, keepdims=True)
        inverse = lax.rsqrt(square * (1.0 / width) + EPSILON)
        normed[:, :half] = (lo * inverse * gain_ref[0]).astype(BF16)
        normed[:, half:] = (hi * inverse * gain_ref[1]).astype(BF16)
        return inverse

    def key_value(normed, kv):
        kv[HALO : HALO + rows, :half] = mm(normed[...], w[1]).astype(BF16)
        kv[HALO : HALO + rows, half:] = mm(normed[...], w[2]).astype(BF16)

    def halo(i, kv):
        return (
            to_patch(i, kv.at[pl.ds(HALO, HALO)], kv.at[pl.ds(HALO + rows, HALO)], before),
            to_patch(i + 1, kv.at[pl.ds(rows, HALO)], kv.at[pl.ds(0, HALO)], after),
        )

    xb_copy.wait()
    xb_send.wait_recv()
    cot_send.start()
    inverse_ref[...] = jnp.broadcast_to(normalize(xb, normed_b), inverse_ref.shape)
    w_copies[1].wait()
    w_copies[2].wait()
    key_value(normed_b, kv_b)
    halo_b = halo(0, kv_b)
    for copy in halo_b:
        copy.start()
    w_copies[0].wait()
    q_b[...] = mm(normed_b[...], w[0]).astype(BF16)

    cot_copy.wait()
    wo_copy.wait()
    cot_send.wait_recv()
    xf_send.start()
    turned_b[...] = normed_b[...].T
    g[...] = (mm_nt(cot[0], wo[:, :half]) + mm_nt(cot[1], wo[:, half:])).astype(BF16)

    lane = lax.broadcasted_iota(jnp.int32, (TILE, 2 * HEAD), 1)
    is_low = lane < HEAD
    low = jnp.where(is_low, 1.0, 0.0).astype(BF16)
    high = jnp.where(is_low, 0.0, 1.0).astype(BF16)

    def stacked(x):
        return jnp.concatenate([x * low, x * high], axis=0)

    def unstacked(x):
        return jnp.where(is_low, x[:TILE], x[TILE:])

    pairs = half // (2 * HEAD)
    steps = rows // TILE * pairs
    scale = HEAD ** (-0.5)

    def places(step):
        row = pl.multiple_of(step // pairs * TILE, TILE)
        col = pl.multiple_of(lax.rem(step, pairs) * (2 * HEAD), 2 * HEAD)
        value_col = pl.multiple_of(half + lax.rem(step, pairs) * (2 * HEAD), 2 * HEAD)
        return row, col, value_col

    def weights_of(q, kv, row, col):
        queries = stacked(q[pl.ds(row, TILE), pl.ds(col, 2 * HEAD)])
        keys = kv[pl.ds(row, WINDOW), pl.ds(col, 2 * HEAD)]
        mask = bias[pl.ds(row, TILE), :]
        scores = mm_nt(queries, keys) * scale + jnp.concatenate([mask, mask], axis=0)
        exponent = jnp.exp(scores - jnp.max(scores, axis=-1, keepdims=True))
        weights = exponent * (1.0 / jnp.sum(exponent, axis=-1, keepdims=True))
        return queries, keys, weights

    for copy in halo_b:
        copy.wait_recv()
    kvg[...] = jnp.zeros_like(kvg)

    def rows_of(c):
        return pl.ds(pl.multiple_of(c * chunk, chunk), chunk)

    def columns_copy(where, source):
        return pltpu.make_async_remote_copy(
            src_ref=turned_b.at[rows_of(where)], dst_ref=columns.at[source],
            send_sem=ns.at[where], recv_sem=nr.at[source],
            device_id={"patch": where}, device_id_type=MESH,
        )

    def columns_start(k, carry):
        columns_copy(lax.rem(p + k, n_patch), p).start()
        return carry

    lax.fori_loop(1, n_patch, columns_start, 0)
    columns[p] = turned_b[rows_of(p)]

    def backward_step(step, carry):
        row, col, value_col = places(step)
        queries, keys, weights = weights_of(q_b, kv_b, row, col)
        values = kv_b[pl.ds(row, WINDOW), pl.ds(value_col, 2 * HEAD)]
        rounded = weights.astype(BF16)
        here = (pl.ds(row, TILE), pl.ds(col, 2 * HEAD))
        att_b[here] = unstacked(mm(rounded, values)).astype(BF16)
        grad_heads = stacked(g[here])
        grad_weights = mm_nt(grad_heads, values)
        inner = jnp.sum(weights * grad_weights, axis=-1, keepdims=True)
        grad_scores = (weights * (grad_weights - inner) * scale).astype(BF16)
        grad_q[here] = unstacked(mm(grad_scores, keys)).astype(BF16)
        kvg[pl.ds(row, WINDOW), pl.ds(col, 2 * HEAD)] += mm_tn(grad_scores, queries)
        kvg[pl.ds(row, WINDOW), pl.ds(value_col, 2 * HEAD)] += mm_tn(rounded, grad_heads)
        return carry

    lax.fori_loop(0, steps, backward_step, 0)

    rim_out[0] = kvg[:HALO].astype(BF16)
    rim_out[1] = kvg[HALO + rows :].astype(BF16)
    rims = (
        to_patch(4, rim_out.at[0], rim_in.at[0], before),
        to_patch(5, rim_out.at[1], rim_in.at[1], after),
    )
    for copy in rims:
        copy.start()

    def sum_copy(d, i, c):
        return pltpu.make_async_remote_copy(
            src_ref=parts.at[i, rows_of(c)], dst_ref=landed.at[d, i, c],
            send_sem=rs_s.at[d, i, c], recv_sem=rs_r.at[d, i, c],
            device_id={"patch": before if d else after}, device_id_type=MESH,
        )

    def sums_first(i):
        @pl.when(p == 0)
        def _():
            def one(k, carry):
                sum_copy(0, i, n_patch - k).start()
                return carry

            lax.fori_loop(1, n_patch, one, 0)

        @pl.when(p == n_patch - 1)
        def _():
            def one(k, carry):
                sum_copy(1, i, k).start()
                return carry

            lax.fori_loop(0, n_patch - 1, one, 0)

    def sums_stage(m):
        right, left = n_patch - 1 - m, m

        def pass_on(d, c):
            for i in range(2):
                copy = sum_copy(d, i, c)
                copy.wait_recv()
                parts[i, rows_of(c)] = (
                    parts[i, rows_of(c)].astype(F32) + landed[d, i, c].astype(F32)
                ).astype(BF16)
                copy.start()

        @pl.when((right > p) & (p > 0))
        def _():
            pass_on(0, right)

        @pl.when((left < p) & (p < n_patch - 1))
        def _():
            pass_on(1, left)

    def block_copy(d, i, j):
        return pltpu.make_async_remote_copy(
            src_ref=gathered.at[i, j], dst_ref=gathered.at[i, j],
            send_sem=ag_s.at[d, i, j], recv_sem=ag_r.at[i, j],
            device_id={"patch": before if d else after}, device_id_type=MESH,
        )

    def block_start(i, j, goes_right, goes_left):
        if goes_right:
            @pl.when(p < n_patch - 1)
            def _():
                block_copy(0, i, j).start()
        if goes_left:
            @pl.when(p > 0)
            def _():
                block_copy(1, i, j).start()

    def blocks_stage(m):
        left, right = p - 1 - m, p + 1 + m

        @pl.when(left >= 0)
        def _():
            for i in range(2):
                block_copy(0, i, left).wait_recv()
                block_start(i, left, True, False)

        @pl.when(right < n_patch)
        def _():
            for i in range(2):
                block_copy(1, i, right).wait_recv()
                block_start(i, right, False, True)

        @pl.when(left >= 0)
        def _():
            for i in range(2):
                gp_ref[1 + i] += mm(columns[left], gathered[i, left])

        @pl.when(right < n_patch)
        def _():
            for i in range(2):
                gp_ref[1 + i] += mm(columns[right], gathered[i, right])

    parts[0, :half] = mm_tn(cot[0], att_b[...]).astype(BF16)
    parts[0, half:] = mm_tn(cot[1], att_b[...]).astype(BF16)
    sums_first(0)
    parts[1] = mm(turned_b[...], grad_q[...]).astype(BF16)
    sums_first(1)

    xf_copy.wait()
    xf_send.wait_recv()
    normalize(xf, normed_f)
    key_value(normed_f, kv_f)
    halo_f = halo(2, kv_f)
    for copy in halo_f:
        copy.start()
    q_f[...] = mm(normed_f[...], w[0]).astype(BF16)

    def forward_step(step, carry):
        row, col, value_col = places(step)
        weights = weights_of(q_f, kv_f, row, col)[2]
        values = kv_f[pl.ds(row, WINDOW), pl.ds(value_col, 2 * HEAD)]
        att_f[pl.ds(row, TILE), pl.ds(col, 2 * HEAD)] = unstacked(
            mm(weights.astype(BF16), values)
        ).astype(BF16)
        return carry

    def forward_half(which):
        return mm(att_f[...], wo[:, pl.ds(pl.multiple_of(which * half, half), half)])

    for copy in rims:
        copy.wait_recv()
    kvg[pl.ds(rows, HALO)] += rim_in[0].astype(F32)
    kvg[pl.ds(HALO, HALO)] += rim_in[1].astype(F32)
    gathered[0, p] = kvg[HALO : HALO + rows, :half].astype(BF16)
    block_start(0, p, True, True)
    gathered[1, p] = kvg[HALO : HALO + rows, half:].astype(BF16)
    block_start(1, p, True, True)

    inverse = inverse_ref[:, :1]

    def normed_half(which):
        d = pl.ds(pl.multiple_of(which * half, half), half)
        return (
            mm_nt(grad_q[...], w[0, d])
            + mm_nt(gathered[0, p], w[1, d])
            + mm_nt(gathered[1, p], w[2, d])
        )

    def unit_half(which):
        return xb[which].astype(F32) * inverse

    away = normed_half(peer)
    gn_out[...] = away.astype(BF16)
    gn_send = to_peer(4, gn_out, gn_in)
    gn_send.start()
    held = normed_half(t)
    gn_own[...] = held
    corr = jnp.sum(away * unit_half(peer) * gain_ref[peer], axis=-1, keepdims=True)
    corr = corr + jnp.sum(held * unit_half(t) * gain_ref[t], axis=-1, keepdims=True)
    corr_row = jnp.broadcast_to(corr, (rows, 128)).T
    corr_out[...] = corr_row[:8]
    corr_send = to_peer(5, corr_out, corr_in)
    corr_send.start()

    def columns_end(k, carry):
        columns_copy(lax.rem(p + k, n_patch), lax.rem(p + k, n_patch)).wait_recv()
        return carry

    lax.fori_loop(1, n_patch, columns_end, 0)
    for i in range(2):
        gp_ref[1 + i] = mm(columns[p], gathered[i, p])

    sums_stage(0)
    for copy in halo_f:
        copy.wait_recv()
    lax.fori_loop(0, steps // 2, forward_step, 0)
    sums_stage(1)
    blocks_stage(0)
    lax.fori_loop(steps // 2, steps, forward_step, 0)
    up_out[...] = forward_half(peer).astype(BF16)
    up_send = to_peer(3, up_out, up_in)
    up_send.start()
    up_own[...] = forward_half(t)

    gn_send.wait_recv()
    corr_send.wait_recv()
    summed = gn_own[...] + gn_in[...].astype(F32)
    unit = unit_half(t)
    row_sum = jnp.broadcast_to((corr_out[...] + corr_in[...])[:1], (128, rows)).T[:, :1]
    change = inverse * (summed * gain_ref[t] - unit * (row_sum * (1.0 / width)))
    bo_out[...] = (cot[t].astype(F32) + change).astype(BF16)
    bo_send = pltpu.make_async_remote_copy(
        src_ref=bo_out, dst_ref=bo_ref, send_sem=ss.at[0], recv_sem=sr.at[0],
        device_id={"section": s_prev}, device_id_type=MESH,
    )
    bo_send.start()
    gain_own = jnp.sum(summed * unit, axis=0, keepdims=True)
    gain_out[...] = jnp.broadcast_to(gain_own, gain_out.shape)

    def gain_copy(k):
        return pltpu.make_async_remote_copy(
            src_ref=gain_out, dst_ref=gain_in.at[k], send_sem=gs.at[k], recv_sem=gr.at[k],
            device_id={"patch": lax.rem(p + k, n_patch)}, device_id_type=MESH,
        )

    def gain_start(k, carry):
        gain_copy(k).start()
        return carry

    lax.fori_loop(1, n_patch, gain_start, 0)

    up_send.wait_recv()
    fo_out[...] = (xf[t].astype(F32) + up_own[...] + up_in[...].astype(F32)).astype(BF16)
    fo_send = pltpu.make_async_remote_copy(
        src_ref=fo_out, dst_ref=fo_ref, send_sem=ss.at[1], recv_sem=sr.at[1],
        device_id={"section": s_next}, device_id_type=MESH,
    )
    fo_send.start()

    def stage(m, carry):
        @pl.when(m + 1 < n_patch - 1)
        def _():
            sums_stage(m + 1)

        blocks_stage(m)
        return carry

    lax.fori_loop(1, n_patch - 1, stage, 0)

    def gain_end(k, total_gain):
        copy = gain_copy(k)
        copy.wait_send()
        copy.wait_recv()
        return total_gain + gain_in[k]

    gg_ref[...] = lax.fori_loop(1, n_patch, gain_end, gain_out[...])[:1]

    for i in range(2):
        held = gp_ref.at[0] if i == 1 else (gn_own.at[pl.ds(0, chunk)] if turned else go_ref)
        held[...] = parts[i, rows_of(p)].astype(F32)

        @pl.when(p > 0)
        def _():
            sum_copy(0, i, p).wait_recv()
            held[...] += landed[0, i, p].astype(F32)

        @pl.when(p < n_patch - 1)
        def _():
            sum_copy(1, i, p).wait_recv()
            held[...] += landed[1, i, p].astype(F32)

    if turned:
        go_ref[...] = gn_own[:chunk].T

    def sent(k, carry):
        where = lax.rem(p + k, n_patch)
        columns_copy(where, p).wait_send()
        return carry

    lax.fori_loop(1, n_patch, sent, 0)

    def passed(c, carry):
        for i in range(2):
            @pl.when((c > p))
            def _():
                sum_copy(0, i, c).wait_send()

            @pl.when((c < p))
            def _():
                sum_copy(1, i, c).wait_send()

            @pl.when((c <= p) & (p < n_patch - 1))
            def _():
                block_copy(0, i, c).wait_send()

            @pl.when((c >= p) & (p > 0))
            def _():
                block_copy(1, i, c).wait_send()
        return carry

    lax.fori_loop(0, n_patch, passed, 0)

    for copy in (xb_send, cot_send, xf_send, gn_send, corr_send, up_send):
        copy.wait_send()
    for copy in halo_b + halo_f + rims:
        copy.wait_send()
    bo_send.wait()
    fo_send.wait()


def move(*refs):
    count = len(refs) // 2
    sources, targets, sems = refs[:count], refs[count : 2 * count], refs[-1]
    copies = [pltpu.make_async_copy(sources[i], targets[i], sems.at[i]) for i in range(count)]
    for copy in copies:
        copy.start()
    for copy in copies:
        copy.wait()


def hand_out(arrays):
    anywhere = pl.BlockSpec(memory_space=pl.ANY)
    return pl.pallas_call(
        move,
        out_shape=tuple(jax.ShapeDtypeStruct(a.shape, a.dtype) for a in arrays),
        in_specs=[anywhere] * len(arrays),
        out_specs=(anywhere,) * len(arrays),
        scratch_shapes=[pltpu.SemaphoreType.DMA((len(arrays),))],
    )(*arrays)


def shards(n_section, n_patch, xf, xb, cot, norm_gain, projection, output_weight, neighbours):
    rows, half = xf.shape[1:]
    width = 2 * half
    chunk = width // n_patch
    turned = chunk % 128 == 0
    anywhere = pl.BlockSpec(memory_space=pl.ANY)
    vmem = pl.BlockSpec(memory_space=pltpu.VMEM)
    block = lambda *shape, dtype=BF16: pltpu.VMEM(shape, dtype)
    dma = pltpu.SemaphoreType.DMA
    outs = pl.pallas_call(
        functools.partial(kernel, n_section, n_patch, turned),
        out_shape=(
            jax.ShapeDtypeStruct((rows, half), BF16),
            jax.ShapeDtypeStruct((rows, half), BF16),
            jax.ShapeDtypeStruct((3, chunk, half), F32),
            jax.ShapeDtypeStruct((half, chunk) if turned else (chunk, half), F32),
            jax.ShapeDtypeStruct((1, half), F32),
        ),
        in_specs=[anywhere, anywhere, anywhere, vmem, anywhere, anywhere, vmem],
        out_specs=(anywhere, anywhere, vmem, vmem, vmem),
        scratch_shapes=[
            block(2, rows, half), block(2, rows, half), block(2, rows, half),
            block(3, width, half), block(half, width), block(rows, WINDOW, dtype=F32),
            block(rows, width), block(rows, width), block(rows, 128, dtype=F32),
            block(rows, half), block(rows, half),
            block(rows + 2 * HALO, width), block(rows + 2 * HALO, width),
            block(rows, half), block(rows, half), block(rows, half), block(rows, half),
            block(rows + 2 * HALO, width, dtype=F32), block(2, HALO, width), block(2, HALO, width),
            block(rows, half, dtype=F32), block(rows, half), block(rows, half),
            block(rows, half, dtype=F32), block(rows, half), block(rows, half),
            block(8, rows, dtype=F32), block(8, rows, dtype=F32),
            block(rows, half), block(rows, half),
            block(2, width, half), block(2, 2, n_patch, chunk, half),
            block(8, half, dtype=F32), block(n_patch, 8, half, dtype=F32),
            block(128, rows, dtype=F32), block(width, rows), block(n_patch, chunk, rows),
            block(2, n_patch, rows, half),
            dma((7,)), dma((6,)), dma((6,)), dma((6,)), dma((6,)), dma((2,)), dma((2,)),
            dma((2, 2, n_patch)), dma((2, 2, n_patch)), dma((2, 2, n_patch)), dma((2, n_patch)),
            dma((n_patch,)), dma((n_patch,)), dma((n_patch,)), dma((n_patch,)),
        ],
        compiler_params=pltpu.CompilerParams(
            collective_id=0, has_side_effects=True, vmem_limit_bytes=56 * 2**20
        ),
        cost_estimate=pl.CostEstimate(flops=6 * 10**9, bytes_accessed=8 * 2**20, transcendentals=10**6),
    )(
        xf[0], xb[0], cot[0], norm_gain[0].reshape(2, 1, half), projection[0], output_weight[0],
        neighbours.T,
    )
    outs = hand_out(outs)
    forward, backward, grad_projection, grad_output, gain = outs
    if not turned:
        grad_output = grad_output.T
    return forward[None], backward[None], grad_projection[None], grad_output[None], gain


def solution(mesh):
    return jax.shard_map(
        functools.partial(shards, mesh.shape["section"], mesh.shape["patch"]),
        mesh=mesh,
        in_specs=(
            P("section", "patch", "tensor"),
            P("section", "patch", "tensor"),
            P("section", "patch", "tensor"),
            P("section", None),
            P("section", None, None, "tensor"),
            P("section", "tensor", None),
            P("patch", None),
        ),
        out_specs=(
            P("section", "patch", "tensor"),
            P("section", "patch", "tensor"),
            P("section", None, "patch", "tensor"),
            P("section", "tensor", "patch"),
            P("section", "tensor"),
        ),
        check_vma=False,
    )
```

```python
import functools

import jax
import jax.numpy as jnp
from jax import lax
from jax.experimental import pallas as pl
from jax.experimental.pallas import tpu as pltpu
from jax.sharding import PartitionSpec as P

HEAD = 64
HALO = 64
TILE = 128
WINDOW = TILE + 2 * HALO
EPSILON = 1e-06
MESH = pl.DeviceIdType.MESH
F32 = jnp.float32
BF16 = jnp.bfloat16


def mm(a, b):
    return lax.dot_general(a, b, (((1,), (0,)), ((), ())), preferred_element_type=F32)


def mm_nt(a, b):
    return lax.dot_general(a, b, (((1,), (1,)), ((), ())), preferred_element_type=F32)


def mm_tn(a, b):
    return lax.dot_general(a, b, (((0,), (0,)), ((), ())), preferred_element_type=F32)


def kernel(
    n_section, n_patch, turned,
    xf_hbm, xb_hbm, cot_hbm, gain_ref, w_hbm, wo_hbm, near_ref,
    fo_ref, bo_ref, gp_ref, go_ref, gg_ref,
    xf, xb, cot, w, wo, bias, normed_b, normed_f, inverse_ref,
    q_b, q_f, kv_b, kv_f, g, att_b, att_f, grad_q, kvg, rim_out, rim_in,
    up_own, up_out, up_in, gn_own, gn_out, gn_in, corr_out, corr_in,
    fo_out, bo_out, parts, landed, gain_out, gain_in, near, turned_b, columns, gathered,
    loc, ts, tr, hs, hr, ss, sr, rs_s, rs_r, ag_s, ag_r, ns, nr, gs, gr,
):
    s, p, t = lax.axis_index("section"), lax.axis_index("patch"), lax.axis_index("tensor")
    peer = 1 - t
    rows, half = xf_hbm.shape
    width = 2 * half
    chunk = width // n_patch
    total = rows * n_patch
    after = lax.rem(p + 1, n_patch)
    before = lax.rem(p + n_patch - 1, n_patch)
    s_next = lax.rem(s + 1, n_section)
    s_prev = lax.rem(s + n_section - 1, n_section)

    w_copies = [pltpu.make_async_copy(w_hbm.at[c], w.at[c], loc.at[c]) for c in range(3)]
    wo_copy = pltpu.make_async_copy(wo_hbm, wo, loc.at[3])
    xb_copy = pltpu.make_async_copy(xb_hbm, xb.at[t], loc.at[4])
    cot_copy = pltpu.make_async_copy(cot_hbm, cot.at[t], loc.at[5])
    xf_copy = pltpu.make_async_copy(xf_hbm, xf.at[t], loc.at[6])
    for copy in (xb_copy, w_copies[1], w_copies[2], w_copies[0], cot_copy, wo_copy, xf_copy):
        copy.start()

    barrier = pltpu.get_barrier_semaphore()
    pl.semaphore_signal(barrier, inc=1, device_id={"tensor": peer}, device_id_type=MESH)
    pl.semaphore_signal(barrier, inc=1, device_id={"section": s_next}, device_id_type=MESH)
    pl.semaphore_signal(barrier, inc=1, device_id={"section": s_prev}, device_id_type=MESH)

    def greet(k, carry):
        pl.semaphore_signal(
            barrier, inc=1, device_id={"patch": lax.rem(p + k, n_patch)}, device_id_type=MESH
        )
        return carry

    lax.fori_loop(1, n_patch, greet, 0)
    pl.semaphore_wait(barrier, 2 + n_patch)

    def to_peer(i, src, dst):
        return pltpu.make_async_remote_copy(
            src_ref=src, dst_ref=dst, send_sem=ts.at[i], recv_sem=tr.at[i],
            device_id={"tensor": peer}, device_id_type=MESH,
        )

    def to_patch(i, src, dst, where):
        return pltpu.make_async_remote_copy(
            src_ref=src, dst_ref=dst, send_sem=hs.at[i], recv_sem=hr.at[i],
            device_id={"patch": where}, device_id_type=MESH,
        )

    xb_send = to_peer(0, xb_hbm, xb.at[t])
    cot_send = to_peer(1, cot_hbm, cot.at[t])
    xf_send = to_peer(2, xf_hbm, xf.at[t])
    xb_send.start()

    first = p * rows - HALO
    tile_start = lax.broadcasted_iota(jnp.int32, (rows, 1), 0) // TILE * TILE
    near[...] = jnp.zeros_like(near)
    near[: near_ref.shape[0], :] = near_ref[...].astype(F32)
    place = near[...].T.astype(jnp.int32) - first
    place = jnp.where(place < 0, place + total, place)
    place = jnp.where(place >= total, place - total, place) - tile_start
    column = lax.broadcasted_iota(jnp.int32, (rows, WINDOW), 1)
    seen = jnp.full((rows, WINDOW), -1e30, F32)
    for k in range(near_ref.shape[0]):
        seen = jnp.where(place[:, k : k + 1] == column, 0.0, seen)
    bias[...] = seen

    def normalize(x, normed):
        lo, hi = x[0].astype(F32), x[1].astype(F32)
        square = jnp.sum(lo * lo, axis=-1, keepdims=True) + jnp.sum(hi * hi, axis=-1, keepdims=True)
        inverse = lax.rsqrt(square * (1.0 / width) + EPSILON)
        normed[:, :half] = (lo * inverse * gain_ref[0]).astype(BF16)
        normed[:, half:] = (hi * inverse * gain_ref[1]).astype(BF16)
        return inverse

    def key_value(normed, kv):
        kv[HALO : HALO + rows, :half] = mm(normed[...], w[1]).astype(BF16)
        kv[HALO : HALO + rows, half:] = mm(normed[...], w[2]).astype(BF16)

    def halo(i, kv):
        return (
            to_patch(i, kv.at[pl.ds(HALO, HALO)], kv.at[pl.ds(HALO + rows, HALO)], before),
            to_patch(i + 1, kv.at[pl.ds(rows, HALO)], kv.at[pl.ds(0, HALO)], after),
        )

    xb_copy.wait()
    xb_send.wait_recv()
    cot_send.start()
    inverse_ref[...] = jnp.broadcast_to(normalize(xb, normed_b), inverse_ref.shape)
    w_copies[1].wait()
    w_copies[2].wait()
    key_value(normed_b, kv_b)
    halo_b = halo(0, kv_b)
    for copy in halo_b:
        copy.start()
    w_copies[0].wait()
    q_b[...] = mm(normed_b[...], w[0]).astype(BF16)

    cot_copy.wait()
    wo_copy.wait()
    cot_send.wait_recv()
    xf_send.start()
    turned_b[...] = normed_b[...].T
    g[...] = (mm_nt(cot[0], wo[:, :half]) + mm_nt(cot[1], wo[:, half:])).astype(BF16)

    lane = lax.broadcasted_iota(jnp.int32, (TILE, 2 * HEAD), 1)
    is_low = lane < HEAD
    low = jnp.where(is_low, 1.0, 0.0).astype(BF16)
    high = jnp.where(is_low, 0.0, 1.0).astype(BF16)

    def stacked(x):
        return jnp.concatenate([x * low, x * high], axis=0)

    def unstacked(x):
        return jnp.where(is_low, x[:TILE], x[TILE:])

    pairs = half // (2 * HEAD)
    steps = rows // TILE * pairs
    scale = HEAD ** (-0.5)

    def places(step):
        row = pl.multiple_of(step // pairs * TILE, TILE)
        col = pl.multiple_of(lax.rem(step, pairs) * (2 * HEAD), 2 * HEAD)
        value_col = pl.multiple_of(half + lax.rem(step, pairs) * (2 * HEAD), 2 * HEAD)
        return row, col, value_col

    def weights_of(q, kv, row, col):
        queries = stacked(q[pl.ds(row, TILE), pl.ds(col, 2 * HEAD)])
        keys = kv[pl.ds(row, WINDOW), pl.ds(col, 2 * HEAD)]
        mask = bias[pl.ds(row, TILE), :]
        scores = mm_nt(queries, keys) * scale + jnp.concatenate([mask, mask], axis=0)
        exponent = jnp.exp(scores - jnp.max(scores, axis=-1, keepdims=True))
        weights = exponent * (1.0 / jnp.sum(exponent, axis=-1, keepdims=True))
        return queries, keys, weights

    for copy in halo_b:
        copy.wait_recv()
    kvg[...] = jnp.zeros_like(kvg)

    def rows_of(c):
        return pl.ds(pl.multiple_of(c * chunk, chunk), chunk)

    def columns_copy(where, source):
        return pltpu.make_async_remote_copy(
            src_ref=turned_b.at[rows_of(where)], dst_ref=columns.at[source],
            send_sem=ns.at[where], recv_sem=nr.at[source],
            device_id={"patch": where}, device_id_type=MESH,
        )

    def columns_start(k, carry):
        columns_copy(lax.rem(p + k, n_patch), p).start()
        return carry

    lax.fori_loop(1, n_patch, columns_start, 0)
    columns[p] = turned_b[rows_of(p)]

    def backward_step(step, carry):
        row, col, value_col = places(step)
        queries, keys, weights = weights_of(q_b, kv_b, row, col)
        values = kv_b[pl.ds(row, WINDOW), pl.ds(value_col, 2 * HEAD)]
        rounded = weights.astype(BF16)
        here = (pl.ds(row, TILE), pl.ds(col, 2 * HEAD))
        att_b[here] = unstacked(mm(rounded, values)).astype(BF16)
        grad_heads = stacked(g[here])
        grad_weights = mm_nt(grad_heads, values)
        inner = jnp.sum(weights * grad_weights, axis=-1, keepdims=True)
        grad_scores = (weights * (grad_weights - inner) * scale).astype(BF16)
        grad_q[here] = unstacked(mm(grad_scores, keys)).astype(BF16)
        kvg[pl.ds(row, WINDOW), pl.ds(col, 2 * HEAD)] += mm_tn(grad_scores, queries)
        kvg[pl.ds(row, WINDOW), pl.ds(value_col, 2 * HEAD)] += mm_tn(rounded, grad_heads)
        return carry

    lax.fori_loop(0, steps, backward_step, 0)

    rim_out[0] = kvg[:HALO].astype(BF16)
    rim_out[1] = kvg[HALO + rows :].astype(BF16)
    rims = (
        to_patch(4, rim_out.at[0], rim_in.at[0], before),
        to_patch(5, rim_out.at[1], rim_in.at[1], after),
    )
    for copy in rims:
        copy.start()

    def sum_copy(d, i, c):
        return pltpu.make_async_remote_copy(
            src_ref=parts.at[i, rows_of(c)], dst_ref=landed.at[d, i, c],
            send_sem=rs_s.at[d, i, c], recv_sem=rs_r.at[d, i, c],
            device_id={"patch": before if d else after}, device_id_type=MESH,
        )

    def sums_first(i):
        @pl.when(p == 0)
        def _():
            def one(k, carry):
                sum_copy(0, i, n_patch - k).start()
                return carry

            lax.fori_loop(1, n_patch, one, 0)

        @pl.when(p == n_patch - 1)
        def _():
            def one(k, carry):
                sum_copy(1, i, k).start()
                return carry

            lax.fori_loop(0, n_patch - 1, one, 0)

    def sums_stage(m):
        right, left = n_patch - 1 - m, m

        def pass_on(d, c):
            for i in range(2):
                copy = sum_copy(d, i, c)
                copy.wait_recv()
                parts[i, rows_of(c)] = (
                    parts[i, rows_of(c)].astype(F32) + landed[d, i, c].astype(F32)
                ).astype(BF16)
                copy.start()

        @pl.when((right > p) & (p > 0))
        def _():
            pass_on(0, right)

        @pl.when((left < p) & (p < n_patch - 1))
        def _():
            pass_on(1, left)

    def block_copy(d, i, j):
        return pltpu.make_async_remote_copy(
            src_ref=gathered.at[i, j], dst_ref=gathered.at[i, j],
            send_sem=ag_s.at[d, i, j], recv_sem=ag_r.at[i, j],
            device_id={"patch": before if d else after}, device_id_type=MESH,
        )

    def block_start(i, j, goes_right, goes_left):
        if goes_right:
            @pl.when(p < n_patch - 1)
            def _():
                block_copy(0, i, j).start()
        if goes_left:
            @pl.when(p > 0)
            def _():
                block_copy(1, i, j).start()

    def blocks_stage(m):
        left, right = p - 1 - m, p + 1 + m

        @pl.when(left >= 0)
        def _():
            for i in range(2):
                block_copy(0, i, left).wait_recv()
                block_start(i, left, True, False)

        @pl.when(right < n_patch)
        def _():
            for i in range(2):
                block_copy(1, i, right).wait_recv()
                block_start(i, right, False, True)

        @pl.when(left >= 0)
        def _():
            for i in range(2):
                gp_ref[1 + i] += mm(columns[left], gathered[i, left])

        @pl.when(right < n_patch)
        def _():
            for i in range(2):
                gp_ref[1 + i] += mm(columns[right], gathered[i, right])

    parts[0, :half] = mm_tn(cot[0], att_b[...]).astype(BF16)
    parts[0, half:] = mm_tn(cot[1], att_b[...]).astype(BF16)
    sums_first(0)
    parts[1] = mm(turned_b[...], grad_q[...]).astype(BF16)
    sums_first(1)

    xf_copy.wait()
    xf_send.wait_recv()
    normalize(xf, normed_f)
    key_value(normed_f, kv_f)
    halo_f = halo(2, kv_f)
    for copy in halo_f:
        copy.start()
    q_f[...] = mm(normed_f[...], w[0]).astype(BF16)

    def forward_step(step, carry):
        row, col, value_col = places(step)
        weights = weights_of(q_f, kv_f, row, col)[2]
        values = kv_f[pl.ds(row, WINDOW), pl.ds(value_col, 2 * HEAD)]
        att_f[pl.ds(row, TILE), pl.ds(col, 2 * HEAD)] = unstacked(
            mm(weights.astype(BF16), values)
        ).astype(BF16)
        return carry

    def forward_half(which):
        return mm(att_f[...], wo[:, pl.ds(pl.multiple_of(which * half, half), half)])

    for copy in rims:
        copy.wait_recv()
    kvg[pl.ds(rows, HALO)] += rim_in[0].astype(F32)
    kvg[pl.ds(HALO, HALO)] += rim_in[1].astype(F32)
    gathered[0, p] = kvg[HALO : HALO + rows, :half].astype(BF16)
    block_start(0, p, True, True)
    gathered[1, p] = kvg[HALO : HALO + rows, half:].astype(BF16)
    block_start(1, p, True, True)

    inverse = inverse_ref[:, :1]

    def normed_half(which):
        d = pl.ds(pl.multiple_of(which * half, half), half)
        return (
            mm_nt(grad_q[...], w[0, d])
            + mm_nt(gathered[0, p], w[1, d])
            + mm_nt(gathered[1, p], w[2, d])
        )

    def unit_half(which):
        return xb[which].astype(F32) * inverse

    away = normed_half(peer)
    gn_out[...] = away.astype(BF16)
    gn_send = to_peer(4, gn_out, gn_in)
    gn_send.start()
    held = normed_half(t)
    gn_own[...] = held
    corr = jnp.sum(away * unit_half(peer) * gain_ref[peer], axis=-1, keepdims=True)
    corr = corr + jnp.sum(held * unit_half(t) * gain_ref[t], axis=-1, keepdims=True)
    corr_row = jnp.broadcast_to(corr, (rows, 128)).T
    corr_out[...] = corr_row[:8]
    corr_send = to_peer(5, corr_out, corr_in)
    corr_send.start()

    def columns_end(k, carry):
        columns_copy(lax.rem(p + k, n_patch), lax.rem(p + k, n_patch)).wait_recv()
        return carry

    lax.fori_loop(1, n_patch, columns_end, 0)
    for i in range(2):
        gp_ref[1 + i] = mm(columns[p], gathered[i, p])

    sums_stage(0)
    for copy in halo_f:
        copy.wait_recv()
    lax.fori_loop(0, steps // 2, forward_step, 0)
    sums_stage(1)
    blocks_stage(0)
    lax.fori_loop(steps // 2, steps, forward_step, 0)
    up_out[...] = forward_half(peer).astype(BF16)
    up_send = to_peer(3, up_out, up_in)
    up_send.start()
    up_own[...] = forward_half(t)

    gn_send.wait_recv()
    corr_send.wait_recv()
    summed = gn_own[...] + gn_in[...].astype(F32)
    unit = unit_half(t)
    row_sum = jnp.broadcast_to((corr_out[...] + corr_in[...])[:1], (128, rows)).T[:, :1]
    change = inverse * (summed * gain_ref[t] - unit * (row_sum * (1.0 / width)))
    bo_out[...] = (cot[t].astype(F32) + change).astype(BF16)
    bo_send = pltpu.make_async_remote_copy(
        src_ref=bo_out, dst_ref=bo_ref, send_sem=ss.at[0], recv_sem=sr.at[0],
        device_id={"section": s_prev}, device_id_type=MESH,
    )
    bo_send.start()
    gain_own = jnp.sum(summed * unit, axis=0, keepdims=True)
    gain_out[...] = jnp.broadcast_to(gain_own, gain_out.shape)

    def gain_copy(k):
        return pltpu.make_async_remote_copy(
            src_ref=gain_out, dst_ref=gain_in.at[k], send_sem=gs.at[k], recv_sem=gr.at[k],
            device_id={"patch": lax.rem(p + k, n_patch)}, device_id_type=MESH,
        )

    def gain_start(k, carry):
        gain_copy(k).start()
        return carry

    lax.fori_loop(1, n_patch, gain_start, 0)

    up_send.wait_recv()
    fo_out[...] = (xf[t].astype(F32) + up_own[...] + up_in[...].astype(F32)).astype(BF16)
    fo_send = pltpu.make_async_remote_copy(
        src_ref=fo_out, dst_ref=fo_ref, send_sem=ss.at[1], recv_sem=sr.at[1],
        device_id={"section": s_next}, device_id_type=MESH,
    )
    fo_send.start()

    def stage(m, carry):
        @pl.when(m + 1 < n_patch - 1)
        def _():
            sums_stage(m + 1)

        blocks_stage(m)
        return carry

    lax.fori_loop(1, n_patch - 1, stage, 0)

    def gain_end(k, total_gain):
        copy = gain_copy(k)
        copy.wait_send()
        copy.wait_recv()
        return total_gain + gain_in[k]

    gg_ref[...] = lax.fori_loop(1, n_patch, gain_end, gain_out[...])[:1]

    for i in range(2):
        held = gp_ref.at[0] if i == 1 else (gn_own.at[pl.ds(0, chunk)] if turned else go_ref)
        held[...] = parts[i, rows_of(p)].astype(F32)

        @pl.when(p > 0)
        def _():
            sum_copy(0, i, p).wait_recv()
            held[...] += landed[0, i, p].astype(F32)

        @pl.when(p < n_patch - 1)
        def _():
            sum_copy(1, i, p).wait_recv()
            held[...] += landed[1, i, p].astype(F32)

    if turned:
        go_ref[...] = gn_own[:chunk].T

    def sent(k, carry):
        where = lax.rem(p + k, n_patch)
        columns_copy(where, p).wait_send()
        return carry

    lax.fori_loop(1, n_patch, sent, 0)

    def passed(c, carry):
        for i in range(2):
            @pl.when((c > p))
            def _():
                sum_copy(0, i, c).wait_send()

            @pl.when((c < p))
            def _():
                sum_copy(1, i, c).wait_send()

            @pl.when((c <= p) & (p < n_patch - 1))
            def _():
                block_copy(0, i, c).wait_send()

            @pl.when((c >= p) & (p > 0))
            def _():
                block_copy(1, i, c).wait_send()
        return carry

    lax.fori_loop(0, n_patch, passed, 0)

    for copy in (xb_send, cot_send, xf_send, gn_send, corr_send, up_send):
        copy.wait_send()
    for copy in halo_b + halo_f + rims:
        copy.wait_send()
    bo_send.wait()
    fo_send.wait()


def move(*refs):
    count = len(refs) // 3
    sources, targets, held, sems = refs[:count], refs[count : 2 * count], refs[2 * count : -1], refs[-1]
    ins = [pltpu.make_async_copy(sources[i], held[i], sems.at[0, i]) for i in range(count)]
    outs = [pltpu.make_async_copy(held[i], targets[i], sems.at[1, i]) for i in range(count)]
    for copy in ins:
        copy.start()
    for i in range(count):
        ins[i].wait()
        outs[i].start()
    for copy in outs:
        copy.wait()


def hand_out(arrays):
    anywhere = pl.BlockSpec(memory_space=pl.ANY)
    return pl.pallas_call(
        move,
        out_shape=tuple(jax.ShapeDtypeStruct(a.shape, a.dtype) for a in arrays),
        in_specs=[anywhere] * len(arrays),
        out_specs=(anywhere,) * len(arrays),
        scratch_shapes=[
            *(pltpu.VMEM(a.shape, a.dtype) for a in arrays),
            pltpu.SemaphoreType.DMA((2, len(arrays))),
        ],
    )(*arrays)


def shards(n_section, n_patch, xf, xb, cot, norm_gain, projection, output_weight, neighbours):
    rows, half = xf.shape[1:]
    width = 2 * half
    chunk = width // n_patch
    turned = chunk % 128 == 0
    anywhere = pl.BlockSpec(memory_space=pl.ANY)
    vmem = pl.BlockSpec(memory_space=pltpu.VMEM)
    block = lambda *shape, dtype=BF16: pltpu.VMEM(shape, dtype)
    dma = pltpu.SemaphoreType.DMA
    outs = pl.pallas_call(
        functools.partial(kernel, n_section, n_patch, turned),
        out_shape=(
            jax.ShapeDtypeStruct((rows, half), BF16),
            jax.ShapeDtypeStruct((rows, half), BF16),
            jax.ShapeDtypeStruct((3, chunk, half), F32),
            jax.ShapeDtypeStruct((half, chunk) if turned else (chunk, half), F32),
            jax.ShapeDtypeStruct((1, half), F32),
        ),
        in_specs=[anywhere, anywhere, anywhere, vmem, anywhere, anywhere, vmem],
        out_specs=(anywhere, anywhere, vmem, vmem, vmem),
        scratch_shapes=[
            block(2, rows, half), block(2, rows, half), block(2, rows, half),
            block(3, width, half), block(half, width), block(rows, WINDOW, dtype=F32),
            block(rows, width), block(rows, width), block(rows, 128, dtype=F32),
            block(rows, half), block(rows, half),
            block(rows + 2 * HALO, width), block(rows + 2 * HALO, width),
            block(rows, half), block(rows, half), block(rows, half), block(rows, half),
            block(rows + 2 * HALO, width, dtype=F32), block(2, HALO, width), block(2, HALO, width),
            block(rows, half, dtype=F32), block(rows, half), block(rows, half),
            block(rows, half, dtype=F32), block(rows, half), block(rows, half),
            block(8, rows, dtype=F32), block(8, rows, dtype=F32),
            block(rows, half), block(rows, half),
            block(2, width, half), block(2, 2, n_patch, chunk, half),
            block(8, half, dtype=F32), block(n_patch, 8, half, dtype=F32),
            block(128, rows, dtype=F32), block(width, rows), block(n_patch, chunk, rows),
            block(2, n_patch, rows, half),
            dma((7,)), dma((6,)), dma((6,)), dma((6,)), dma((6,)), dma((2,)), dma((2,)),
            dma((2, 2, n_patch)), dma((2, 2, n_patch)), dma((2, 2, n_patch)), dma((2, n_patch)),
            dma((n_patch,)), dma((n_patch,)), dma((n_patch,)), dma((n_patch,)),
        ],
        compiler_params=pltpu.CompilerParams(
            collective_id=0, has_side_effects=True, vmem_limit_bytes=56 * 2**20
        ),
        cost_estimate=pl.CostEstimate(flops=6 * 10**9, bytes_accessed=8 * 2**20, transcendentals=10**6),
    )(
        xf[0], xb[0], cot[0], norm_gain[0].reshape(2, 1, half), projection[0], output_weight[0],
        neighbours.T,
    )
    outs = hand_out(outs)
    forward, backward, grad_projection, grad_output, gain = outs
    if not turned:
        grad_output = grad_output.T
    return forward[None], backward[None], grad_projection[None], grad_output[None], gain


def solution(mesh):
    return jax.shard_map(
        functools.partial(shards, mesh.shape["section"], mesh.shape["patch"]),
        mesh=mesh,
        in_specs=(
            P("section", "patch", "tensor"),
            P("section", "patch", "tensor"),
            P("section", "patch", "tensor"),
            P("section", None),
            P("section", None, None, "tensor"),
            P("section", "tensor", None),
            P("patch", None),
        ),
        out_specs=(
            P("section", "patch", "tensor"),
            P("section", "patch", "tensor"),
            P("section", None, "patch", "tensor"),
            P("section", "tensor", "patch"),
            P("section", "tensor"),
        ),
        check_vma=False,
    )
```
